32 devices in a mesh: dp: 4 (over y, x), region: 8 (over z, core).
Axes of the slice: x: 2, y: 2, z: 4, core: 2. Of those that a mesh axis runs over, the one named last changes fastest.
Arguments:
- leaves: float32 [128, 64, 1024], P('region', None, 'dp'), may hold values from -280 to 0
- weights: float32 [2, 128, 8, 64, 64], P(None, 'region'), may hold values from 0.00048828125 to 0.0078125
- groups: int32 [2, 8, 8, 2], P(None, None, 'region'), may hold values from 0 to 15
- prod_kids: int32 [2, 256, 2], P(None, 'region'), may hold values from 0 to 15
- sum_kids: int32 [2, 128, 8], P(None, 'region'), may hold values from 0 to 31
- cotangent: float32 [128, 64, 1024], P('region', None, 'dp'), may hold values from -6 to 6
Outputs:
- top_logp: float32 [128, 64, 1024], P('region', None, 'dp')
- leaf_grad: float32 [128, 64, 1024], P('region', None, 'dp')
- weight_flow: float32 [2, 128, 8, 64, 64], P(None, 'region')
The draws below stay inside these ranges and needn't reach their ends.
All inputs are finite; a program needn't handle non-finite values.
Results may differ from the reference program's by a relative error of at most 0.0003.
Values sent between devices are 32-bit elements; how exact they have to be, the bound alone decides.
A program may use at most 128 MiB of HBM per device.

```python
import math
import jax
import jax.numpy as jnp
from jax import lax

BLOCK = 64
B_DEV = 16
K = 8
G = 2
PAIRS = 2
P_DEV = 32
SLOTS = 16
NBLK = 128
SAMPLES = 1024
N_REGION = 8


def draw_leaves(key, part):
    second = jax.random.fold_in(key, 1)
    shape = (NBLK, BLOCK, SAMPLES)
    values = -6.0 * jax.random.uniform(second, shape, jnp.float32)
    return values.astype(jnp.float32)


def set_ends(array, key, smallest, top_value):
    index_at = [jax.random.randint(jax.random.fold_in(key, axis), (), 0, length) for axis, length in enumerate(array.shape)]
    widest = array.shape.index(max(array.shape))
    beside = index_at[:widest] + [(index_at[widest] + 1) % array.shape[widest]] + index_at[widest + 1:]
    return array.at[tuple(index_at)].set(smallest).at[tuple(beside)].set(top_value)


def level_of(stream_key, shape, shards, low, high):
    factor_of = 1.0
    for axis_at, shards_of in shards:
        heights = jax.random.uniform(jax.random.fold_in(jax.random.fold_in(stream_key, 6), axis_at), (shards_of,), jnp.float32, low / len(shards), high / len(shards))
        factor_of = factor_of * jnp.repeat(jnp.exp(heights), shape[axis_at] // shards_of).reshape((-1,) + (1,) * (len(shape) - 1 - axis_at))
    return factor_of


def noise(rng, dims, spread, limit, cuts=(), kind=jnp.bfloat16):
    result = spread * jax.random.normal(rng, dims, jnp.float32)
    if cuts:
        result = result * level_of(rng, dims, cuts, -0.22, 0.18)
    return jnp.clip(result, -limit, limit).astype(kind)


def setup_inputs(seed: int = 0) -> dict:
    keys = jax.random.split(jax.random.key(seed), 7)
    return {
        "leaves": draw_leaves(jax.random.fold_in(keys[6], 71), 0),
        "weights": jnp.clip(jnp.exp(math.log(0.0078125) - 2.7725887 * jax.random.uniform(keys[1], (PAIRS, NBLK, K, BLOCK, BLOCK), jnp.float32) ** level_of(keys[1], (PAIRS, NBLK, K, BLOCK, BLOCK), ((1, 8),), -0.2, 0.2)), 0.00048828125, 0.0078125),
        "groups": set_ends(jax.random.randint(keys[2], (PAIRS, N_REGION, N_REGION, G), 0, B_DEV), jax.random.fold_in(keys[2], 1), 0, B_DEV - 1).astype(jnp.int32),
        "prod_kids": set_ends(jax.random.randint(keys[3], (PAIRS, N_REGION * P_DEV, 2), 0, SLOTS), jax.random.fold_in(keys[3], 1), 0, SLOTS - 1).astype(jnp.int32),
        "sum_kids": set_ends(jax.random.randint(keys[4], (PAIRS, NBLK, K), 0, P_DEV), jax.random.fold_in(keys[4], 1), 0, P_DEV - 1).astype(jnp.int32),
        "cotangent": noise(keys[5], (NBLK, BLOCK, SAMPLES), 1.0, 6.0, ((0, 8), (2, 4)), jnp.float32),
    }


def reader_layer(level_in, slot_src, kid_pairs, sum_list, weight_part):
    gathered = level_in[slot_src]
    prods = gathered[kid_pairs[:, 0]] + gathered[kid_pairs[:, 1]]
    chosen = prods[sum_list]
    shift_top = lax.stop_gradient(lax.optimization_barrier(jnp.max(chosen, axis=(1, 2), keepdims=True)))
    exponent = jnp.exp(chosen - shift_top)
    running_totals = jnp.einsum('bkij,bkjs->bis', weight_part, exponent, precision=lax.Precision.HIGHEST)
    return shift_top[:, 0] + jnp.log(running_totals)

def layer(level_in, group_ids, kid_all, sum_all, weight_complete):
    source_offset = (jnp.arange(N_REGION, dtype=jnp.int32) * B_DEV)[None, :, None]
    slot_src = (group_ids + source_offset).reshape(N_REGION, SLOTS).astype(jnp.int32)

    def stepper(items):
        return reader_layer(level_in, items[0], items[1], items[2], items[3])
    outputs = lax.map(jax.checkpoint(stepper), (slot_src, kid_all.reshape(N_REGION, P_DEV, 2), sum_all.reshape(N_REGION, B_DEV, K), weight_complete.reshape(N_REGION, B_DEV, K, BLOCK, BLOCK)))
    return outputs.reshape(NBLK, BLOCK, SAMPLES)

def reference(leaves, weights, groups, prod_kids, sum_kids, cotangent):

    def forward(level_in, weight_complete):
        for level in range(PAIRS):
            level_in = layer(level_in, groups[level], prod_kids[level], sum_kids[level], weight_complete[level])
        return level_in
    top_logp, pullback = jax.vjp(forward, leaves, weights)
    leaf_grad, weight_grad = pullback(cotangent)
    return (top_logp, leaf_grad, weight_grad / SAMPLES)
```

```python
import functools

import jax
import jax.numpy as jnp
from jax import lax
from jax.experimental import pallas as pl
from jax.experimental.pallas import tpu as pltpu
from jax.sharding import PartitionSpec as P

F32, BF16 = jnp.float32, jnp.bfloat16
SMEM = pl.BlockSpec(memory_space=pltpu.SMEM)
VMEM = pl.BlockSpec(memory_space=pltpu.VMEM)
ANY = pl.BlockSpec(memory_space=pl.ANY)
LIMIT = 56 * 2**20


def params():
    return pltpu.CompilerParams(vmem_limit_bytes=LIMIT)


def cost(flops, nbytes, exps=0):
    return pl.CostEstimate(flops=flops, bytes_accessed=nbytes, transcendentals=exps)


def halves(x):
    high = x.astype(BF16)
    return high, (x - high.astype(F32)).astype(BF16)


def dot(a, b, dims):
    return lax.dot_general(a, b, (dims, ((), ())), preferred_element_type=F32)


def make_prods(level, kids, taken, prods, tops):
    count = prods.shape[0]

    def step(p, _):
        at = (level * count + p) * 2
        value = taken[kids[at]] + taken[kids[at + 1]]
        prods[p] = value
        tops[p] = jnp.max(value, axis=0, keepdims=True)
        return _

    lax.fori_loop(0, count, step, 0, unroll=2)


def chosen_ids(level, lists, b, blocks, kinds):
    return [lists[(level * blocks + b) * kinds + k] for k in range(kinds)]


def shift_of(ids, tops):
    shift = tops[ids[0]]
    for i in ids[1:]:
        shift = jnp.maximum(shift, tops[i])
    return shift


def expo_of(ids, prods, shift):
    return jnp.concatenate([jnp.exp(prods[i] - shift) for i in ids], axis=0)


def wide_weights(weights, b):
    return jnp.concatenate([weights[b, k] for k in range(weights.shape[1])], axis=1)


def totals_of(w_high, w_low, e_high, e_low):
    rows = w_high.shape[0]
    both = dot(jnp.concatenate([w_high, w_low], axis=0), e_high, ((1,), (0,)))
    return both[:rows] + both[rows:] + dot(w_high, e_low, ((1,), (0,)))


def flow_of(r_high, r_low, e_high, e_low):
    rows = r_high.shape[0]
    both = dot(jnp.concatenate([r_high, r_low], axis=0), e_high, ((1,), (1,)))
    return both[:rows] + both[rows:] + dot(r_high, e_low, ((1,), (1,)))


def chosen_grad(w_high, w_low, r_high, r_low, expo):
    left = jnp.concatenate([w_high, w_low, w_high], axis=0)
    right = jnp.concatenate([r_high, r_high, r_low], axis=0)
    return dot(left, right, ((0,), (0,))) * expo


def add_chosen(ids, grad, prod_grad):
    rows = prod_grad.shape[1]
    for k, i in enumerate(ids):
        prod_grad[i] += grad[k * rows : (k + 1) * rows]


def to_slots(level, kids, prod_grad, slot_grad):
    slot_grad[...] = jnp.zeros_like(slot_grad)
    count = prod_grad.shape[0]

    def step(p, _):
        at = (level * count + p) * 2
        value = prod_grad[p]
        slot_grad[kids[at]] += value
        slot_grad[kids[at + 1]] += value
        return _

    lax.fori_loop(0, count, step, 0)


def home(level, group_ids, sent, grad):
    slots = sent.shape[0]
    grad[...] = jnp.zeros_like(grad)

    def step(i, _):
        grad[group_ids[level * slots + i]] += sent[i]
        return _

    lax.fori_loop(0, slots, step, 0)


def pick_kernel(level, group_ids, source, out, sems):
    slots = out.shape[0]
    copies = [
        pltpu.make_async_copy(
            source.at[group_ids[level * slots + i]], out.at[i], sems.at[i]
        )
        for i in range(slots)
    ]
    for c in copies:
        c.start()
    for c in copies:
        c.wait()


def forward_kernel(level, group_ids, kids, lists, taken, weights, outgoing, totals, prods, tops, level_out):
    blocks, kinds = weights.shape[:2]
    make_prods(level, kids, taken, prods, tops)

    def step(b, _):
        ids = chosen_ids(level, lists, b, blocks, kinds)
        shift = shift_of(ids, tops)
        e = halves(expo_of(ids, prods, shift))
        w = halves(wide_weights(weights, b))
        total = totals_of(*w, *e)
        totals[b] = total
        level_out[b] = shift + jnp.log(total)
        return _

    lax.fori_loop(0, blocks, step, 0, unroll=2)
    slots = outgoing.shape[0]

    def send(i, _):
        outgoing[i] = level_out[group_ids[(level + 1) * slots + i]]
        return _

    lax.fori_loop(0, slots, send, 0)


def top_kernel(level, scale, kids, lists, taken, weights, cotangent, top, slot_grad, flow, prods, tops, prod_grad):
    blocks, kinds = weights.shape[:2]
    make_prods(level, kids, taken, prods, tops)
    prod_grad[...] = jnp.zeros_like(prod_grad)

    def step(b, _):
        ids = chosen_ids(level, lists, b, blocks, kinds)
        shift = shift_of(ids, tops)
        expo = expo_of(ids, prods, shift)
        e = halves(expo)
        w = halves(wide_weights(weights, b))
        total = totals_of(*w, *e)
        top[b] = shift + jnp.log(total)
        r = halves(cotangent[b] / total)
        flow[b] = flow_of(*r, *e) * scale
        add_chosen(ids, chosen_grad(*w, *r, expo), prod_grad)
        return _

    lax.fori_loop(0, blocks, step, 0, unroll=2)
    to_slots(level, kids, prod_grad, slot_grad)


def flow_kernel(level, scale, group_ids, kids, lists, taken, totals, sent, ratio, flow, prods, tops, grad):
    blocks = totals.shape[0]
    kinds = flow.shape[2] // flow.shape[1]
    home(level + 1, group_ids, sent, grad)
    make_prods(level, kids, taken, prods, tops)

    def step(b, _):
        ids = chosen_ids(level, lists, b, blocks, kinds)
        e = halves(expo_of(ids, prods, shift_of(ids, tops)))
        value = grad[b] / totals[b]
        ratio[b] = value
        flow[b] = flow_of(*halves(value), *e) * scale
        return _

    lax.fori_loop(0, blocks, step, 0, unroll=2)


def slots_kernel(level, kids, lists, taken, weights, ratio, slot_grad, prods, tops, prod_grad):
    blocks, kinds = weights.shape[:2]
    make_prods(level, kids, taken, prods, tops)
    prod_grad[...] = jnp.zeros_like(prod_grad)

    def step(b, _):
        ids = chosen_ids(level, lists, b, blocks, kinds)
        expo = expo_of(ids, prods, shift_of(ids, tops))
        w = halves(wide_weights(weights, b))
        add_chosen(ids, chosen_grad(*w, *halves(ratio[b]), expo), prod_grad)
        return _

    lax.fori_loop(0, blocks, step, 0, unroll=2)
    to_slots(level, kids, prod_grad, slot_grad)


def home_kernel(level, group_ids, sent, grad):
    home(level, group_ids, sent, grad)


def unfold_kernel(flow, *rest):
    out = rest[-1]
    rows = flow.shape[1]

    for k in range(out.shape[1]):
        out[0, k] = flow[0, :, k * rows : (k + 1) * rows]


def unfold(level, levels, kinds, flow, base=None):
    blocks, rows, _ = flow.shape
    given = [] if base is None else [base]
    return pl.pallas_call(
        unfold_kernel,
        grid=(blocks,),
        out_shape=jax.ShapeDtypeStruct((levels, blocks, kinds, rows, rows), F32),
        in_specs=[pl.BlockSpec((1, rows, kinds * rows), lambda b: (b, 0, 0))] + [ANY] * len(given),
        out_specs=pl.BlockSpec((None, 1, kinds, rows, rows), lambda b: (level, b, 0, 0, 0)),
        input_output_aliases={1: 0} if given else {},
        compiler_params=params(),
        cost_estimate=cost(0, 6 * 2**20),
        name="unfold",
    )(flow, *given)


def swap(x):
    return lax.all_to_all(x, "region", split_axis=0, concat_axis=0, tiled=True)


def per_device(leaves, weights, groups, prod_kids, sum_kids, cotangent):
    levels, blocks, kinds, rows, _ = weights.shape
    columns = leaves.shape[2]
    slots = groups.shape[1] * groups.shape[3]
    count = prod_kids.shape[1]
    scale = 1.0 / (columns * lax.axis_size("dp"))
    group_ids, kids, lists = groups.reshape(-1), prod_kids.reshape(-1), sum_kids.reshape(-1)

    def shape(*dims):
        return jax.ShapeDtypeStruct(dims, F32)

    taken_like, level_like = shape(slots, rows, columns), shape(blocks, rows, columns)
    flow_like = shape(blocks, rows, kinds * rows)
    prod_scratch = [
        pltpu.VMEM((count, rows, columns), F32),
        pltpu.VMEM((count, 1, columns), F32),
    ]
    prod_grad = pltpu.VMEM((count, rows, columns), F32)
    macs = blocks * rows * rows * kinds * columns
    expos = blocks * kinds * rows * columns
    mib = 2**20

    def call(kernel, outs, scratch, amount, *args, specs, name, out_specs=None):
        return pl.pallas_call(
            kernel,
            out_shape=outs,
            in_specs=specs,
            out_specs=out_specs or jax.tree.map(lambda _: VMEM, outs),
            scratch_shapes=scratch,
            compiler_params=params(),
            cost_estimate=amount,
            name=name,
        )(*args)

    outgoing = call(
        functools.partial(pick_kernel, 0), taken_like, [pltpu.SemaphoreType.DMA((slots,))],
        cost(0, 2 * mib), group_ids, leaves, specs=[SMEM, ANY], out_specs=ANY, name="pick",
    )
    kept = []
    for level in range(levels - 1):
        taken = swap(outgoing)
        outgoing, totals = call(
            functools.partial(forward_kernel, level), (taken_like, level_like),
            prod_scratch + [pltpu.VMEM((blocks, rows, columns), F32)],
            cost(24 * macs, 8 * mib, expos), group_ids, kids, lists, taken, weights[level],
            specs=[SMEM] * 3 + [VMEM] * 2, name="forward",
        )
        kept.append((taken, totals))
    level = levels - 1
    taken = swap(outgoing)
    top, slot_grad, flow = call(
        functools.partial(top_kernel, level, scale), (level_like, taken_like, flow_like),
        prod_scratch + [prod_grad], cost(72 * macs, 12 * mib, expos),
        kids, lists, taken, weights[level], cotangent,
        specs=[SMEM] * 2 + [VMEM] * 3, name="top",
    )
    sent = swap(slot_grad)
    flow = lax.psum(flow, "dp")
    weight_flow = unfold(level, levels, kinds, flow)
    for level in reversed(range(levels - 1)):
        taken, totals = kept[level]
        ratio, part = call(
            functools.partial(flow_kernel, level, scale), (level_like, flow_like),
            prod_scratch + [pltpu.VMEM((blocks, rows, columns), F32)],
            cost(24 * macs, 8 * mib, expos), group_ids, kids, lists, taken, totals, sent,
            specs=[SMEM] * 3 + [VMEM] * 3, name="flow",
        )
        part, flow = lax.optimization_barrier((part, flow))
        slot_grad = call(
            functools.partial(slots_kernel, level), taken_like, prod_scratch + [prod_grad],
            cost(24 * macs, 8 * mib, expos), kids, lists, taken, weights[level], ratio,
            specs=[SMEM] * 2 + [VMEM] * 3, name="slots",
        )
        sent = swap(slot_grad)
        flow = lax.psum(part, "dp")
        weight_flow = unfold(level, levels, kinds, flow, weight_flow)
    leaf_grad = call(
        functools.partial(home_kernel, 0), level_like, [], cost(0, 2 * mib), group_ids, sent,
        specs=[SMEM, VMEM], name="home",
    )
    return top, leaf_grad, weight_flow


def solution(mesh):
    placed = (
        P("region", None, "dp"),
        P(None, "region", None, None, None),
        P(None, None, "region", None),
        P(None, "region", None),
        P(None, "region", None),
        P("region", None, "dp"),
    )
    return jax.shard_map(
        per_device,
        mesh=mesh,
        in_specs=placed,
        out_specs=(
            P("region", None, "dp"),
            P("region", None, "dp"),
            P(None, "region", None, None, None),
        ),
        check_vma=False,
    )
```

```python
import functools

import jax
import jax.numpy as jnp
from jax import lax
from jax.experimental import pallas as pl
from jax.experimental.pallas import tpu as pltpu
from jax.sharding import PartitionSpec as P

F32, BF16 = jnp.float32, jnp.bfloat16
SMEM = pl.BlockSpec(memory_space=pltpu.SMEM)
VMEM = pl.BlockSpec(memory_space=pltpu.VMEM)
ANY = pl.BlockSpec(memory_space=pl.ANY)
LIMIT = 56 * 2**20


def params():
    return pltpu.CompilerParams(vmem_limit_bytes=LIMIT)


def cost(flops, nbytes, exps=0):
    return pl.CostEstimate(flops=flops, bytes_accessed=nbytes, transcendentals=exps)


def halves(x):
    high = x.astype(BF16)
    return high, (x - high.astype(F32)).astype(BF16)


def dot(a, b, dims):
    return lax.dot_general(a, b, (dims, ((), ())), preferred_element_type=F32)


def make_prods(level, kids, taken, prods, tops):
    count = prods.shape[0]

    def step(p, _):
        at = (level * count + p) * 2
        value = taken[kids[at]] + taken[kids[at + 1]]
        prods[p] = value
        tops[p] = jnp.max(value, axis=0, keepdims=True)
        return _

    lax.fori_loop(0, count, step, 0, unroll=2)


def chosen_ids(level, lists, b, blocks, kinds):
    return [lists[(level * blocks + b) * kinds + k] for k in range(kinds)]


def shift_of(ids, tops):
    shift = tops[ids[0]]
    for i in ids[1:]:
        shift = jnp.maximum(shift, tops[i])
    return shift


def expo_of(ids, prods, shift):
    return jnp.concatenate([jnp.exp(prods[i] - shift) for i in ids], axis=0)


def wide_weights(weights, b):
    return jnp.concatenate([weights[b, k] for k in range(weights.shape[1])], axis=1)


def totals_of(w_high, w_low, e_high, e_low):
    rows = w_high.shape[0]
    both = dot(jnp.concatenate([w_high, w_low], axis=0), e_high, ((1,), (0,)))
    return both[:rows] + both[rows:] + dot(w_high, e_low, ((1,), (0,)))


def flow_of(r_high, r_low, e_high, e_low):
    rows = r_high.shape[0]
    both = dot(jnp.concatenate([r_high, r_low], axis=0), e_high, ((1,), (1,)))
    return both[:rows] + both[rows:] + dot(r_high, e_low, ((1,), (1,)))


def chosen_grad(w_high, w_low, r_high, r_low, expo):
    left = jnp.concatenate([w_high, w_low, w_high], axis=0)
    right = jnp.concatenate([r_high, r_high, r_low], axis=0)
    return dot(left, right, ((0,), (0,))) * expo


def add_chosen(ids, grad, prod_grad):
    rows = prod_grad.shape[1]
    for k, i in enumerate(ids):
        prod_grad[i] += grad[k * rows : (k + 1) * rows]


def to_slots(level, kids, prod_grad, slot_grad):
    slot_grad[...] = jnp.zeros_like(slot_grad)
    count = prod_grad.shape[0]

    def step(p, _):
        at = (level * count + p) * 2
        value = prod_grad[p]
        slot_grad[kids[at]] += value
        slot_grad[kids[at + 1]] += value
        return _

    lax.fori_loop(0, count, step, 0)


def home(level, group_ids, sent, grad):
    slots = sent.shape[0]
    grad[...] = jnp.zeros_like(grad)

    def step(i, _):
        grad[group_ids[level * slots + i]] += sent[i]
        return _

    lax.fori_loop(0, slots, step, 0)


def pick_kernel(level, group_ids, source, out, sems):
    slots = out.shape[0]
    copies = [
        pltpu.make_async_copy(
            source.at[group_ids[level * slots + i]], out.at[i], sems.at[i]
        )
        for i in range(slots)
    ]
    for c in copies:
        c.start()
    for c in copies:
        c.wait()


def forward_kernel(level, group_ids, kids, lists, taken, all_weights, outgoing, totals, prods, tops, level_out, weights, sem):
    arriving = pltpu.make_async_copy(all_weights.at[level], weights, sem)
    arriving.start()
    blocks, kinds = weights.shape[:2]
    make_prods(level, kids, taken, prods, tops)
    arriving.wait()

    def step(b, _):
        ids = chosen_ids(level, lists, b, blocks, kinds)
        shift = shift_of(ids, tops)
        e = halves(expo_of(ids, prods, shift))
        w = halves(wide_weights(weights, b))
        total = totals_of(*w, *e)
        totals[b] = total
        level_out[b] = shift + jnp.log(total)
        return _

    lax.fori_loop(0, blocks, step, 0, unroll=2)
    slots = outgoing.shape[0]

    def send(i, _):
        outgoing[i] = level_out[group_ids[(level + 1) * slots + i]]
        return _

    lax.fori_loop(0, slots, send, 0)


def top_kernel(level, scale, kids, lists, taken, all_weights, cotangent, top, slot_grad, flow, prods, tops, prod_grad, weights, sem):
    arriving = pltpu.make_async_copy(all_weights.at[level], weights, sem)
    arriving.start()
    blocks, kinds = weights.shape[:2]
    make_prods(level, kids, taken, prods, tops)
    prod_grad[...] = jnp.zeros_like(prod_grad)
    arriving.wait()

    def step(b, _):
        ids = chosen_ids(level, lists, b, blocks, kinds)
        shift = shift_of(ids, tops)
        expo = expo_of(ids, prods, shift)
        e = halves(expo)
        w = halves(wide_weights(weights, b))
        total = totals_of(*w, *e)
        top[b] = shift + jnp.log(total)
        r = halves(cotangent[b] / total)
        flow[b] = flow_of(*r, *e) * scale
        add_chosen(ids, chosen_grad(*w, *r, expo), prod_grad)
        return _

    lax.fori_loop(0, blocks, step, 0, unroll=2)
    to_slots(level, kids, prod_grad, slot_grad)


def flow_kernel(level, scale, group_ids, kids, lists, taken, totals, sent, ratio, flow, prods, tops, grad):
    blocks = totals.shape[0]
    kinds = flow.shape[2] // flow.shape[1]
    home(level + 1, group_ids, sent, grad)
    make_prods(level, kids, taken, prods, tops)

    def step(b, _):
        ids = chosen_ids(level, lists, b, blocks, kinds)
        e = halves(expo_of(ids, prods, shift_of(ids, tops)))
        value = grad[b] / totals[b]
        ratio[b] = value
        flow[b] = flow_of(*halves(value), *e) * scale
        return _

    lax.fori_loop(0, blocks, step, 0, unroll=2)


def slots_kernel(level, kids, lists, taken, all_weights, ratio, slot_grad, prods, tops, prod_grad, weights, sem):
    arriving = pltpu.make_async_copy(all_weights.at[level], weights, sem)
    arriving.start()
    blocks, kinds = weights.shape[:2]
    make_prods(level, kids, taken, prods, tops)
    prod_grad[...] = jnp.zeros_like(prod_grad)
    arriving.wait()

    def step(b, _):
        ids = chosen_ids(level, lists, b, blocks, kinds)
        expo = expo_of(ids, prods, shift_of(ids, tops))
        w = halves(wide_weights(weights, b))
        add_chosen(ids, chosen_grad(*w, *halves(ratio[b]), expo), prod_grad)
        return _

    lax.fori_loop(0, blocks, step, 0, unroll=2)
    to_slots(level, kids, prod_grad, slot_grad)


def home_kernel(level, group_ids, sent, grad):
    home(level, group_ids, sent, grad)


def unfold_kernel(level, count, owners, *refs):
    shares, (out, folded, sems) = refs[:count], refs[-3:]
    width, rows, _ = shares[0].shape
    copies = []
    for s, share in enumerate(shares):
        for k in range(folded.shape[2]):
            folded[s, :, k] = share[:, :, k * rows : (k + 1) * rows]
        to = out.at[level, pl.ds(owners[s] * width, width)]
        copies.append(pltpu.make_async_copy(folded.at[s], to, sems.at[s]))
        copies[-1].start()
    for c in copies:
        c.wait()


def unfold(level, levels, kinds, summed, base=None):
    shares, owners = summed
    count = len(shares)
    width, rows, _ = shares[0].shape
    given = [] if base is None else [base]
    return pl.pallas_call(
        functools.partial(unfold_kernel, level, count),
        out_shape=jax.ShapeDtypeStruct((levels, width * count, kinds, rows, rows), F32),
        in_specs=[SMEM] + [VMEM] * count + [ANY] * len(given),
        out_specs=ANY,
        scratch_shapes=[
            pltpu.VMEM((count, width, kinds, rows, rows), F32),
            pltpu.SemaphoreType.DMA((count,)),
        ],
        input_output_aliases={count + 1: 0} if given else {},
        compiler_params=params(),
        cost_estimate=cost(0, 6 * 2**20),
        name="unfold",
    )(owners, *shares, *given)


def swap(x):
    return lax.all_to_all(x, "region", split_axis=0, concat_axis=0, tiled=True)


def target(i, step, size):
    return i ^ step if size & (size - 1) == 0 else (i + step) % size


def source(i, step, size):
    return i ^ step if size & (size - 1) == 0 else (i - step) % size


def hand(x, step, size):
    return lax.ppermute(x, "dp", [(i, target(i, step, size)) for i in range(size)])


def dp_sum(flow):
    size, me = lax.axis_size("dp"), lax.axis_index("dp")
    width = flow.shape[0] // size

    def part(owner):
        return lax.dynamic_slice_in_dim(flow, owner * width, width, 0)

    parts = [hand(part(target(me, s, size)), s, size) for s in range(1, size)]
    share = part(me)
    for p in parts:
        share = share + p
    owners = jnp.stack([me] + [source(me, s, size) for s in range(1, size)])
    return [share] + [hand(share, s, size) for s in range(1, size)], owners


def per_device(leaves, weights, groups, prod_kids, sum_kids, cotangent):
    levels, blocks, kinds, rows, _ = weights.shape
    columns = leaves.shape[2]
    slots = groups.shape[1] * groups.shape[3]
    count = prod_kids.shape[1]
    scale = 1.0 / (columns * lax.axis_size("dp"))
    group_ids, kids, lists = groups.reshape(-1), prod_kids.reshape(-1), sum_kids.reshape(-1)

    def shape(*dims):
        return jax.ShapeDtypeStruct(dims, F32)

    taken_like, level_like = shape(slots, rows, columns), shape(blocks, rows, columns)
    flow_like = shape(blocks, rows, kinds * rows)
    prod_scratch = [
        pltpu.VMEM((count, rows, columns), F32),
        pltpu.VMEM((count, 1, columns), F32),
    ]
    prod_grad = pltpu.VMEM((count, rows, columns), F32)
    macs = blocks * rows * rows * kinds * columns
    expos = blocks * kinds * rows * columns
    mib = 2**20

    weight_scratch = [pltpu.VMEM(weights.shape[1:], F32), pltpu.SemaphoreType.DMA]

    def call(kernel, outs, scratch, amount, *args, specs, name, out_specs=None):
        return pl.pallas_call(
            kernel,
            out_shape=outs,
            in_specs=specs,
            out_specs=out_specs or jax.tree.map(lambda _: VMEM, outs),
            scratch_shapes=scratch,
            compiler_params=params(),
            cost_estimate=amount,
            name=name,
        )(*args)

    outgoing = call(
        functools.partial(pick_kernel, 0), taken_like, [pltpu.SemaphoreType.DMA((slots,))],
        cost(0, 2 * mib), group_ids, leaves, specs=[SMEM, ANY], name="pick",
    )
    kept = []
    for level in range(levels - 1):
        taken = swap(outgoing)
        outgoing, totals = call(
            functools.partial(forward_kernel, level), (taken_like, level_like),
            prod_scratch + [pltpu.VMEM((blocks, rows, columns), F32)] + weight_scratch,
            cost(24 * macs, 8 * mib, expos), group_ids, kids, lists, taken, weights,
            specs=[SMEM] * 3 + [VMEM, ANY], name="forward",
        )
        kept.append((taken, totals))
    level = levels - 1
    taken = swap(outgoing)
    top, slot_grad, flow = call(
        functools.partial(top_kernel, level, scale), (level_like, taken_like, flow_like),
        prod_scratch + [prod_grad] + weight_scratch, cost(72 * macs, 12 * mib, expos),
        kids, lists, taken, weights, cotangent,
        specs=[SMEM] * 2 + [VMEM, ANY, VMEM], name="top",
    )
    sent = swap(slot_grad)
    flow = dp_sum(flow)
    weight_flow = unfold(level, levels, kinds, flow)
    for level in reversed(range(levels - 1)):
        taken, totals = kept[level]
        ratio, part = call(
            functools.partial(flow_kernel, level, scale), (level_like, flow_like),
            prod_scratch + [pltpu.VMEM((blocks, rows, columns), F32)],
            cost(24 * macs, 8 * mib, expos), group_ids, kids, lists, taken, totals, sent,
            specs=[SMEM] * 3 + [VMEM] * 3, name="flow",
        )
        slot_grad = call(
            functools.partial(slots_kernel, level), taken_like, prod_scratch + [prod_grad] + weight_scratch,
            cost(24 * macs, 8 * mib, expos), kids, lists, taken, weights, ratio,
            specs=[SMEM] * 2 + [VMEM, ANY, VMEM], name="slots",
        )
        sent = swap(slot_grad)
        flow = dp_sum(part)
        weight_flow = unfold(level, levels, kinds, flow, weight_flow)
    leaf_grad = call(
        functools.partial(home_kernel, 0), level_like, [], cost(0, 2 * mib), group_ids, sent,
        specs=[SMEM, VMEM], name="home",
    )
    return top, leaf_grad, weight_flow


def solution(mesh):
    placed = (
        P("region", None, "dp"),
        P(None, "region", None, None, None),
        P(None, None, "region", None),
        P(None, "region", None),
        P(None, "region", None),
        P("region", None, "dp"),
    )
    return jax.shard_map(
        per_device,
        mesh=mesh,
        in_specs=placed,
        out_specs=(
            P("region", None, "dp"),
            P("region", None, "dp"),
            P(None, "region", None, None, None),
        ),
        check_vma=False,
    )
```
